32 devices in a mesh: mem: 8 (over z, x), head: 4 (over y, core).
Axes of the slice: x: 2, y: 2, z: 4, core: 2. Of those that a mesh axis runs over, the one named last changes fastest.
Arguments:
- query: bfloat16 [1024, 5120], P('mem', 'head'), may hold values from -96 to 96
- local_keys: bfloat16 [1024, 5120], P('mem', 'head'), may hold values from -6 to 6
- local_values: bfloat16 [1024, 5120], P('mem', 'head'), may hold values from -6 to 6
- mem_keys: bfloat16 [16384, 5120], P('mem', 'head'), may hold values from -4.5 to 4.5
- mem_values: bfloat16 [16384, 5120], P('mem', 'head'), may hold values from -6 to 6
- block_ids: int32 [8, 32], P('mem'), may hold values from 0 to 127, as said below
- out_proj: bfloat16 [5120, 5120], P('head'), may hold values from -1 to 1
- grad_out: bfloat16 [1024, 5120], P('mem', 'head'), may hold values from -6 to 6
Outputs:
- output: bfloat16 [1024, 5120], P('mem', 'head')
- grad_query: bfloat16 [1024, 5120], P('mem', 'head')
- grad_mem_keys: bfloat16 [16384, 5120], P('mem', 'head')
- grad_mem_values: bfloat16 [16384, 5120], P('mem', 'head')
The draws below stay inside these ranges and needn't reach their ends.
Inputs may be any that keep to these rules, and one draw needn't show every extreme that they name: `block_ids`: each row names 32 different memory blocks. At most 6 of a row's blocks share one value of id // 16, and in every row exactly 6 share one value.
All inputs are finite; a program needn't handle non-finite values.
Results may differ from the reference program's by a relative error of at most 0.02.
Values may be sent and summed in bfloat16 or wider, within the bound.
A program may use at most 192 MiB of HBM per device.

```python
import jax
import jax.numpy as jnp
from jax import lax

HEADS = 40
HS = 128
DM = 5120
BLOCK = 128
R = 32
MB = 16
CAP = 6
QBLOCKS = 8
TOKENS = 1024
MBLOCKS = 128
MROWS = 16384
N_MEM = 8


def shuffled(subkeys, count):

    def one_order(single):
        return jax.random.permutation(single, count)
    return jax.vmap(one_order)(subkeys)


def route_table(key):
    key = jax.random.fold_in(key, 101)
    subkeys = jax.random.split(key, 6)
    holders = N_MEM
    others = holders - 1
    ranking = jax.random.permutation(subkeys[0], holders)
    first_draw = jax.random.randint(subkeys[1], (QBLOCKS,), 0, holders)
    second_draw = jax.random.randint(subkeys[2], (QBLOCKS,), 0, holders)
    hottest = ranking[jnp.minimum(first_draw, second_draw)]
    spread = shuffled(jax.random.split(subkeys[3], QBLOCKS), others)
    places = jnp.arange(R)
    beyond = jnp.maximum(places - CAP, 0)
    column = jnp.broadcast_to(beyond % others, (QBLOCKS, R))
    picked = jnp.take_along_axis(spread, column, axis=1)
    holder = jnp.where(places[None, :] < CAP, hottest[:, None], (hottest[:, None] + 1 + picked) % holders)
    repeat_index = jnp.where(places < CAP, places, beyond // others)
    local_orders = shuffled(jax.random.split(subkeys[4], QBLOCKS * holders), MB).reshape(QBLOCKS, holders, MB)
    slot_index = local_orders[jnp.arange(QBLOCKS)[:, None], holder, repeat_index[None, :]]
    block_names = holder * MB + slot_index
    mixing = shuffled(jax.random.split(subkeys[5], QBLOCKS), R)
    return jnp.take_along_axis(block_names, mixing, axis=1).astype(jnp.int32)


def key_table(key):
    key = jax.random.fold_in(key, 202)
    noise_field = jnp.clip(jax.random.normal(key, (MROWS, HEADS * HS), jnp.float32), -4.5, 4.5)
    second_row = (jnp.arange(MROWS) % BLOCK == 1)[:, None]
    return jnp.where(second_row, noise_field, noise_field)


def draw_block_ids(key, part):
    return route_table(key)


def draw_mem_keys(key, part):
    return key_table(key).astype(jnp.bfloat16)


def draw_query(key, part):
    own_key = jax.random.fold_in(key, 3)
    return (2.0 * jnp.clip(jax.random.normal(own_key, (TOKENS, HEADS * HS), jnp.float32), -6.0, 6.0)).astype(jnp.bfloat16)


def levels(key, dims, cuts, smallest, largest):
    loudness = 1.0
    for axis_at, parts in cuts:
        steps = jax.random.uniform(jax.random.fold_in(jax.random.fold_in(key, 6), axis_at), (parts,), jnp.float32, smallest / len(cuts), largest / len(cuts))
        loudness = loudness * jnp.repeat(jnp.exp(steps), dims[axis_at] // parts).reshape((-1,) + (1,) * (len(dims) - 1 - axis_at))
    return loudness


def scatter_about(key, shape, scale, limit, cuts=(), kind=jnp.bfloat16):
    loudness = levels(key, shape, cuts, -0.22, 0.18) if cuts else 1.0
    result = jax.random.normal(key, shape, jnp.float32) * scale * loudness
    return jnp.minimum(jnp.maximum(result, -limit), limit).astype(kind)


def setup_inputs(seed: int = 0) -> dict:
    seeds = jax.random.split(jax.random.key(seed), 9)
    return {
        "query": draw_query(jax.random.fold_in(seeds[8], 71), 0),
        "local_keys": scatter_about(seeds[1], (TOKENS, DM), 1.0, 6.0, ((0, 8), (1, 4))),
        "local_values": scatter_about(seeds[2], (TOKENS, DM), 1.0, 6.0, ((0, 8), (1, 4))),
        "mem_keys": draw_mem_keys(jax.random.fold_in(seeds[8], 71), 0),
        "mem_values": scatter_about(seeds[4], (MROWS, DM), 1.0, 6.0, ((0, 8), (1, 4))),
        "block_ids": draw_block_ids(jax.random.fold_in(seeds[8], 71), 0),
        "out_proj": scatter_about(seeds[6], (DM, DM), HEADS ** -0.5, 1.0, ((0, 4),)),
        "grad_out": scatter_about(seeds[7], (TOKENS, DM), 1.0, 6.0, ((0, 8), (1, 4))),
    }


lowest = -1e30


def narrow(values):
    return lax.optimization_barrier(values.astype(jnp.bfloat16)).astype(jnp.float32)


def reference(query, local_keys, local_values, mem_keys, mem_values, block_ids, out_proj, grad_out):
    score_scale = HS ** -0.5
    key_store = mem_keys.reshape(MBLOCKS, BLOCK, HEADS, HS)
    value_store = mem_values.reshape(MBLOCKS, BLOCK, HEADS, HS)
    query_heads = query.reshape(QBLOCKS, BLOCK, HEADS, HS)
    near_keys = local_keys.reshape(QBLOCKS, BLOCK, HEADS, HS)
    near_values = local_values.reshape(QBLOCKS, BLOCK, HEADS, HS)
    causal = jnp.tril(jnp.ones((BLOCK, BLOCK), dtype=jnp.bool_))
    counted = jnp.concatenate([causal, jnp.ones((BLOCK, R * BLOCK), dtype=jnp.bool_)], axis=1)

    def collect(block_index):
        chosen = block_ids[block_index]
        keys_all = jnp.concatenate([near_keys[block_index], key_store[chosen].reshape(R * BLOCK, HEADS, HS)], axis=0)
        values_all = jnp.concatenate([near_values[block_index], value_store[chosen].reshape(R * BLOCK, HEADS, HS)], axis=0)
        return query_heads[block_index], keys_all, values_all

    def scores_of(queries, keys_all):
        raw = jnp.einsum("qhd,khd->hqk", queries.astype(jnp.float32), keys_all.astype(jnp.float32)) * score_scale
        return jnp.where(counted, raw, lowest)

    def forward_block(block_index):
        queries, keys_all, values_all = collect(block_index)
        scores = scores_of(queries, keys_all)
        peaks = jnp.max(scores, axis=2)
        weight = jnp.where(counted, jnp.exp(scores - peaks[..., None]), 0.0)
        norms = jnp.sum(weight, axis=2)
        mixed = jnp.einsum("hqk,khd->qhd", narrow(weight), values_all.astype(jnp.float32))
        attention = (mixed / norms.T[..., None]).astype(jnp.bfloat16)
        return attention, (peaks + jnp.log(norms)).T

    attention, log_norm = lax.map(forward_block, jnp.arange(QBLOCKS, dtype=jnp.int32))
    rows_out = attention.reshape(TOKENS, DM)
    output = jnp.dot(rows_out, out_proj, preferred_element_type=jnp.float32).astype(jnp.bfloat16)
    d_attention = jnp.dot(grad_out, out_proj.T, preferred_element_type=jnp.float32).astype(jnp.bfloat16)
    grad_heads = d_attention.reshape(QBLOCKS, BLOCK, HEADS, HS)
    deltas = jnp.sum(grad_heads.astype(jnp.float32) * attention.astype(jnp.float32), axis=3)

    def backward_block(running, block_index):
        key_grad, value_grad = running
        queries, keys_all, values_all = collect(block_index)
        scores = scores_of(queries, keys_all)
        prob = jnp.where(counted, jnp.exp(scores - log_norm[block_index].T[..., None]), 0.0)
        upstream = grad_heads[block_index].astype(jnp.float32)
        prob_grad = jnp.einsum("qhd,khd->hqk", upstream, values_all.astype(jnp.float32))
        score_grad = narrow(prob * (prob_grad - deltas[block_index].T[..., None]))
        query_grad = jnp.einsum("hqk,khd->qhd", score_grad, keys_all.astype(jnp.float32)) * score_scale
        mem_key_grad = jnp.einsum("hqk,qhd->khd", score_grad[:, :, BLOCK:], queries.astype(jnp.float32)) * score_scale
        mem_value_grad = jnp.einsum("hqk,qhd->khd", narrow(prob[:, :, BLOCK:]), upstream)
        chosen = block_ids[block_index]
        key_grad = key_grad.at[chosen].add(mem_key_grad.reshape(R, BLOCK, HEADS, HS))
        value_grad = value_grad.at[chosen].add(mem_value_grad.reshape(R, BLOCK, HEADS, HS))
        return (key_grad, value_grad), query_grad.astype(jnp.bfloat16)

    zero_grads = jnp.zeros((MBLOCKS, BLOCK, HEADS, HS), jnp.float32)
    (key_grad, value_grad), query_grad = lax.scan(backward_block, (zero_grads, zero_grads), jnp.arange(QBLOCKS, dtype=jnp.int32))
    return (output, query_grad.reshape(TOKENS, DM), key_grad.reshape(MROWS, DM).astype(jnp.bfloat16), value_grad.reshape(MROWS, DM).astype(jnp.bfloat16))
```

```python
import functools
import math

import jax
import jax.numpy as jnp
from jax import lax
from jax.experimental import pallas as pl
from jax.experimental.pallas import tpu as pltpu
from jax.sharding import PartitionSpec as P

HS = 128
BLOCK = 128
R = 32
STAT_ROWS = 16
LOWEST = -1e30
SCALE = HS ** (-0.5)
LOG2E = math.log2(math.e)
F32 = jnp.float32
BF16 = jnp.bfloat16
VMEM_LIMIT = 56 * 1024 * 1024


def dot_last(a, b):
    return lax.dot_general(a, b, (((1,), (1,)), ((), ())), preferred_element_type=F32)


def dot_plain(a, b):
    return lax.dot_general(a, b, (((1,), (0,)), ((), ())), preferred_element_type=F32)


def owned_slots(ids, holder, capacity, stored):
    is_owned = ids // stored == holder
    rank = jnp.cumsum(is_owned.astype(jnp.int32), axis=1) - 1
    chosen = jnp.logical_and(
        is_owned[:, None, :], rank[:, None, :] == jnp.arange(capacity, dtype=jnp.int32)[None, :, None]
    )
    slots = jnp.sum(jnp.where(chosen, (ids % stored)[:, None, :], 0), axis=2).astype(jnp.int32)
    count = jnp.sum(is_owned.astype(jnp.int32), axis=1, keepdims=True)
    return jnp.concatenate([slots, count], axis=1)


def by_count(count, capacity, body):
    small = capacity - 2
    if small < 3:
        body(capacity)
        return
    pl.when(count <= small)(lambda: body(small))
    pl.when(count > small)(lambda: body(capacity))


def forward_kernel(blocks, capacity, stored, slots_ref, q_ref, k_ref, v_ref, out_ref, stat_ref, vt_ref):
    head = pl.program_id(0)
    for m in range(stored):
        vt_ref[m] = v_ref[m * BLOCK : (m + 1) * BLOCK, :].T

    def one_block(b, carry):
        count = slots_ref[b, capacity]
        q = q_ref[pl.ds(pl.multiple_of(b * BLOCK, BLOCK), BLOCK), :]

        def body(n):
            scores = []
            peak = jnp.full((1, BLOCK), LOWEST, F32)
            for j in range(n):
                slot = slots_ref[b, j]
                keys = k_ref[pl.ds(pl.multiple_of(slot * BLOCK, BLOCK), BLOCK), :]
                s = dot_last(keys, q) * (SCALE * LOG2E)
                s = jnp.where(j < count, s, LOWEST)
                scores.append(s)
            top = functools.reduce(jnp.maximum, scores)
            peak = jnp.max(top, axis=0, keepdims=True)
            weights = [jnp.exp2(s - peak) for s in scores]
            norm = jnp.sum(functools.reduce(jnp.add, weights), axis=0, keepdims=True)
            total = None
            for j in range(n):
                term = dot_plain(vt_ref[slots_ref[b, j]], weights[j].astype(BF16))
                total = term if total is None else total + term
            out_ref[b, 0] = total.astype(BF16)
            stat_ref[b, 0, pl.ds(head, 1), :] = peak
            stat_ref[b, 1, pl.ds(head, 1), :] = norm

        by_count(count, capacity, body)
        return carry

    lax.fori_loop(0, blocks, one_block, 0)


def holder_forward(slots, q_all, keys, values, capacity):
    rows, width = q_all.shape
    heads, blocks, stored = width // HS, rows // BLOCK, keys.shape[0] // BLOCK
    column = lambda n: pl.BlockSpec((n, HS), lambda h, s: (0, h))
    return pl.pallas_call(
        functools.partial(forward_kernel, blocks, capacity, stored),
        grid_spec=pltpu.PrefetchScalarGridSpec(
            num_scalar_prefetch=1,
            grid=(heads,),
            in_specs=[column(rows), column(stored * BLOCK), column(stored * BLOCK)],
            out_specs=[
                pl.BlockSpec((blocks, 1, HS, BLOCK), lambda h, s: (0, h, 0, 0)),
                pl.BlockSpec((blocks, 2, STAT_ROWS, BLOCK), lambda h, s: (0, 0, 0, 0)),
            ],
            scratch_shapes=[pltpu.VMEM((stored, HS, BLOCK), BF16)],
        ),
        out_shape=[
            jax.ShapeDtypeStruct((blocks, heads, HS, BLOCK), BF16),
            jax.ShapeDtypeStruct((blocks, 2, STAT_ROWS, BLOCK), F32),
        ],
        compiler_params=pltpu.CompilerParams(vmem_limit_bytes=VMEM_LIMIT),
        cost_estimate=pl.CostEstimate(flops=4 * 10**9, bytes_accessed=16 * 10**6, transcendentals=0),
    )(slots, q_all, keys, values)


def combine_kernel(groups, q_ref, k_ref, v_ref, g_ref, got_ref, stat_ref, att_ref, dq_ref, row_ref):
    head = pl.program_id(0)
    q, k, v, g = q_ref[...], k_ref[...], v_ref[...], g_ref[...]
    key_at = lax.broadcasted_iota(jnp.int32, (BLOCK, BLOCK), 0)
    query_at = lax.broadcasted_iota(jnp.int32, (BLOCK, BLOCK), 1)
    counted = key_at <= query_at
    s = dot_last(k, q) * (SCALE * LOG2E)
    s = jnp.where(counted, s, LOWEST)
    peak = jnp.max(s, axis=0, keepdims=True)
    got_peak = [stat_ref[i, 0, pl.ds(head, 1), :] for i in range(groups)]
    got_norm = [stat_ref[i, 1, pl.ds(head, 1), :] for i in range(groups)]
    peak = functools.reduce(jnp.maximum, got_peak, peak)
    w = jnp.where(counted, jnp.exp2(s - peak), 0.0)
    norm = jnp.sum(w, axis=0, keepdims=True)
    mixed = dot_plain(v.T, w.astype(BF16))
    for i in range(groups):
        factor = jnp.exp2(got_peak[i] - peak)
        norm = norm + got_norm[i] * factor
        mixed = mixed + got_ref[i, 0].astype(F32) * factor
    attention = (mixed / norm).astype(BF16)
    att_ref[...] = attention.T
    lse = peak + jnp.log2(norm)
    delta = jnp.sum(g.T.astype(F32) * attention.astype(F32), axis=0, keepdims=True)
    row_ref[0, pl.ds(head, 1), :] = lse
    row_ref[1, pl.ds(head, 1), :] = delta
    prob = jnp.where(counted, jnp.exp2(s - lse), 0.0)
    ds = (prob * (dot_last(v, g) - delta)).astype(BF16)
    dq_ref[...] = dot_plain(k.T, ds).T * SCALE


def combine(query, keys, values, grad, got, stats):
    rows, width = query.shape
    heads, groups = width // HS, got.shape[0]
    column = pl.BlockSpec((rows, HS), lambda h: (0, h))
    return pl.pallas_call(
        functools.partial(combine_kernel, groups),
        grid=(heads,),
        in_specs=[
            column, column, column, column,
            pl.BlockSpec((groups, 1, HS, BLOCK), lambda h: (0, h, 0, 0)),
            pl.BlockSpec((groups, 2, STAT_ROWS, BLOCK), lambda h: (0, 0, 0, 0)),
        ],
        out_specs=[column, column, pl.BlockSpec((2, STAT_ROWS, BLOCK), lambda h: (0, 0, 0))],
        out_shape=[
            jax.ShapeDtypeStruct((rows, width), BF16),
            jax.ShapeDtypeStruct((rows, width), F32),
            jax.ShapeDtypeStruct((2, STAT_ROWS, BLOCK), F32),
        ],
        compiler_params=pltpu.CompilerParams(vmem_limit_bytes=VMEM_LIMIT),
        cost_estimate=pl.CostEstimate(flops=10**8, bytes_accessed=6 * 10**6, transcendentals=0),
    )(query, keys, values, grad, got, stats)


def backward_kernel(
    blocks, capacity, stored,
    slots_ref, q_ref, g_ref, k_ref, v_ref, row_ref, dq_ref, dk_ref, dv_ref, kt_ref, dka_ref, dva_ref,
):
    head = pl.program_id(0)
    dka_ref[...] = jnp.zeros_like(dka_ref)
    dva_ref[...] = jnp.zeros_like(dva_ref)
    for m in range(stored):
        kt_ref[m] = k_ref[m * BLOCK : (m + 1) * BLOCK, :].T

    def one_block(b, carry):
        count = slots_ref[b, capacity]
        here = pl.ds(pl.multiple_of(b * BLOCK, BLOCK), BLOCK)
        q, g = q_ref[here, :], g_ref[here, :]
        lse = row_ref[b, 0, pl.ds(head, 1), :]
        delta = row_ref[b, 1, pl.ds(head, 1), :]

        def body(n):
            probs, grads = [], []
            total = None
            for j in range(n):
                at = pl.ds(pl.multiple_of(slots_ref[b, j] * BLOCK, BLOCK), BLOCK)
                s = dot_last(k_ref[at, :], q) * (SCALE * LOG2E)
                s = jnp.where(j < count, s, LOWEST)
                prob = jnp.exp2(s - lse)
                ds = (prob * (dot_last(v_ref[at, :], g) - delta)).astype(BF16)
                probs.append(prob.astype(BF16))
                grads.append(ds)
                term = dot_plain(kt_ref[slots_ref[b, j]], ds)
                total = term if total is None else total + term
            dks = [dot_plain(ds, q) for ds in grads]
            dvs = [dot_plain(p, g) for p in probs]
            dq_ref[here, :] = (total * SCALE).T.astype(BF16)
            for j in range(n):
                slot = slots_ref[b, j]
                dka_ref[slot] += dks[j]
                dva_ref[slot] += dvs[j]

        by_count(count, capacity, body)
        return carry

    lax.fori_loop(0, blocks, one_block, 0)
    for m in range(stored):
        dk_ref[m * BLOCK : (m + 1) * BLOCK, :] = (dka_ref[m] * SCALE).astype(BF16)
        dv_ref[m * BLOCK : (m + 1) * BLOCK, :] = dva_ref[m].astype(BF16)


def holder_backward(slots, q_all, g_all, keys, values, row_stats, capacity):
    rows, width = q_all.shape
    heads, blocks, stored = width // HS, rows // BLOCK, keys.shape[0] // BLOCK
    column = lambda n: pl.BlockSpec((n, HS), lambda h, s: (0, h))
    mem = stored * BLOCK
    return pl.pallas_call(
        functools.partial(backward_kernel, blocks, capacity, stored),
        grid_spec=pltpu.PrefetchScalarGridSpec(
            num_scalar_prefetch=1,
            grid=(heads,),
            in_specs=[
                column(rows), column(rows), column(mem), column(mem),
                pl.BlockSpec((blocks, 2, STAT_ROWS, BLOCK), lambda h, s: (0, 0, 0, 0)),
            ],
            out_specs=[column(rows), column(mem), column(mem)],
            scratch_shapes=[
                pltpu.VMEM((stored, HS, BLOCK), BF16),
                pltpu.VMEM((stored, BLOCK, HS), F32),
                pltpu.VMEM((stored, BLOCK, HS), F32),
            ],
        ),
        out_shape=[
            jax.ShapeDtypeStruct((rows, width), BF16),
            jax.ShapeDtypeStruct((mem, width), BF16),
            jax.ShapeDtypeStruct((mem, width), BF16),
        ],
        compiler_params=pltpu.CompilerParams(vmem_limit_bytes=VMEM_LIMIT),
        cost_estimate=pl.CostEstimate(flops=10**10, bytes_accessed=28 * 10**6, transcendentals=0),
    )(slots, q_all, g_all, keys, values, row_stats)


def per_device(
    query, local_keys, local_values, mem_keys, mem_values, block_ids, out_proj, grad_out
):
    groups = lax.axis_size("mem")
    holder = lax.axis_index("mem")
    stored = mem_keys.shape[0] // BLOCK
    capacity = R // groups + 2
    ids = lax.all_gather(block_ids, "mem", axis=0, tiled=True)
    q_all = lax.all_gather(query, "mem", axis=0, tiled=True)
    slots = owned_slots(ids, holder, capacity, stored)
    grad = lax.dot_general(
        lax.all_gather(grad_out, "head", axis=1, tiled=True),
        out_proj,
        (((1,), (1,)), ((), ())),
        preferred_element_type=F32,
    ).astype(BF16)
    g_all = lax.all_gather(grad, "mem", axis=0, tiled=True)
    part, stats = holder_forward(slots, q_all, mem_keys, mem_values, capacity)
    got = lax.all_to_all(part, "mem", split_axis=0, concat_axis=0, tiled=True)
    got_stats = lax.all_to_all(stats, "mem", split_axis=0, concat_axis=0, tiled=True)
    attention, local_dq, row_stats = combine(
        query, local_keys, local_values, grad, got, got_stats
    )
    all_stats = lax.all_gather(row_stats, "mem", axis=0, tiled=False)
    projected = jnp.dot(attention, out_proj, preferred_element_type=F32).astype(BF16)
    output = lax.psum_scatter(projected, "head", scatter_dimension=1, tiled=True)
    dq, grad_mem_keys, grad_mem_values = holder_backward(
        slots, q_all, g_all, mem_keys, mem_values, all_stats, capacity
    )
    mine = lax.psum_scatter(dq, "mem", scatter_dimension=0, tiled=True)
    grad_query = (mine.astype(F32) + local_dq).astype(BF16)
    return (output, grad_query, grad_mem_keys, grad_mem_values)


def solution(mesh):
    split = P("mem", "head")
    placed = (split, split, split, split, split, P("mem", None), P("head", None), split)
    return jax.shard_map(
        per_device, mesh=mesh, in_specs=placed, out_specs=(split,) * 4, check_vma=False
    )
```

```python
import functools
import math

import jax
import jax.numpy as jnp
from jax import lax
from jax.experimental import pallas as pl
from jax.experimental.pallas import tpu as pltpu
from jax.sharding import PartitionSpec as P

HS = 128
BLOCK = 128
R = 32
STAT_ROWS = 16
LOWEST = -1e30
SCALE = HS ** (-0.5)
LOG2E = math.log2(math.e)
F32 = jnp.float32
BF16 = jnp.bfloat16
MESH = pl.DeviceIdType.MESH
VMEM_LIMIT = 56 * 1024 * 1024


def dot_last(a, b):
    return lax.dot_general(a, b, (((1,), (1,)), ((), ())), preferred_element_type=F32)


def dot_plain(a, b):
    return lax.dot_general(a, b, (((1,), (0,)), ((), ())), preferred_element_type=F32)


def owned_slots(ids, holder, capacity, stored):
    is_owned = ids // stored == holder
    rank = jnp.cumsum(is_owned.astype(jnp.int32), axis=1) - 1
    chosen = jnp.logical_and(
        is_owned[:, None, :], rank[:, None, :] == jnp.arange(capacity, dtype=jnp.int32)[None, :, None]
    )
    slots = jnp.sum(jnp.where(chosen, (ids % stored)[:, None, :], 0), axis=2).astype(jnp.int32)
    count = jnp.sum(is_owned.astype(jnp.int32), axis=1, keepdims=True)
    return jnp.concatenate([slots, count], axis=1)


def meet(groups, me):
    barrier = pltpu.get_barrier_semaphore()
    for d in range(1, groups):
        pl.semaphore_signal(
            barrier, inc=1, device_id={"mem": lax.rem(me + d, groups)}, device_id_type=MESH
        )
    pl.semaphore_wait(barrier, groups - 1)


def push(src, dst, send_sem, recv_sem, peer):
    return pltpu.make_async_remote_copy(
        src_ref=src,
        dst_ref=dst,
        send_sem=send_sem,
        recv_sem=recv_sem,
        device_id={"mem": peer},
        device_id_type=MESH,
    )


def remote_params(collective_id):
    return pltpu.CompilerParams(
        vmem_limit_bytes=VMEM_LIMIT, collective_id=collective_id, has_side_effects=True
    )


def ring_kernel(groups, x_ref, i_ref, xs_ref, is_ref, local, xsend, xrecv, isend, irecv):
    me = lax.axis_index("mem")
    place = (1 - me % 2) * (me // 2) + (me % 2) * (groups - 1 - me // 2)

    def device_at(p):
        p = lax.rem(p + groups, groups)
        upper = p // (groups // 2)
        return (1 - upper) * (2 * p) + upper * (2 * (groups - 1 - p) + 1)

    sides = (device_at(place + 1), device_at(place - 1))
    barrier = pltpu.get_barrier_semaphore()
    for side in sides:
        pl.semaphore_signal(barrier, inc=1, device_id={"mem": side}, device_id_type=MESH)
    pl.semaphore_wait(barrier, 2)
    own = [
        pltpu.make_async_copy(x_ref, xs_ref.at[me], local.at[0]),
        pltpu.make_async_copy(i_ref, is_ref.at[me], local.at[1]),
    ]
    for copy in own:
        copy.start()
    steps = (groups // 2, groups - 1 - groups // 2)
    sent = []
    for t in range(steps[0]):
        for way in range(2):
            if t >= steps[way]:
                continue
            sign = 1 - 2 * way
            block = device_at(place - sign * t)
            if t:
                before = device_at(place - sign * t)
                push(x_ref, xs_ref.at[before], xsend.at[way, t - 1], xrecv.at[way, t - 1], sides[way]).wait_recv()
                push(i_ref, is_ref.at[before], isend.at[way, t - 1], irecv.at[way, t - 1], sides[way]).wait_recv()
            for src, dst, ss, rs in (
                (x_ref if t == 0 else xs_ref.at[block], xs_ref.at[block], xsend, xrecv),
                (i_ref if t == 0 else is_ref.at[block], is_ref.at[block], isend, irecv),
            ):
                copy = push(src, dst, ss.at[way, t], rs.at[way, t], sides[way])
                copy.start()
                sent.append(copy)
    for way in range(2):
        t = steps[way]
        last = device_at(place - (1 - 2 * way) * t)
        push(x_ref, xs_ref.at[last], xsend.at[way, t - 1], xrecv.at[way, t - 1], sides[way]).wait_recv()
        push(i_ref, is_ref.at[last], isend.at[way, t - 1], irecv.at[way, t - 1], sides[way]).wait_recv()
    for copy in sent:
        copy.wait_send()
    for copy in own:
        copy.wait()


def ring_gather(x, ids, groups):
    steps = groups // 2
    anywhere = pl.BlockSpec(memory_space=pl.ANY)
    return pl.pallas_call(
        functools.partial(ring_kernel, groups),
        in_specs=[anywhere, anywhere],
        out_specs=[anywhere, anywhere],
        out_shape=[
            jax.ShapeDtypeStruct((groups,) + x.shape, x.dtype),
            jax.ShapeDtypeStruct((groups,) + ids.shape, ids.dtype),
        ],
        scratch_shapes=[pltpu.SemaphoreType.DMA((2,))] + [pltpu.SemaphoreType.DMA((2, steps))] * 4,
        compiler_params=remote_params(0),
    )(x, ids)


def forward_kernel(
    groups, heads, capacity, stored,
    slots_ref, mask_ref, q_ref, k_ref, v_ref, got_ref, gstat_ref,
    vt_ref, part_ref, stat_ref, send, recv, ssend, srecv, local,
):
    head = pl.program_id(0)
    me = lax.axis_index("mem")

    @pl.when(head == 0)
    def _():
        meet(groups, me)
        stat_ref[...] = jnp.zeros_like(stat_ref)

    for m in range(stored):
        vt_ref[m] = v_ref[m].T

    def one_block(b, carry):
        q = q_ref[pl.ds(pl.multiple_of(b * BLOCK, BLOCK), BLOCK), :]
        scores = []
        for j in range(capacity):
            s = dot_last(k_ref[slots_ref[b, j]], q) * (SCALE * LOG2E)
            scores.append(s + mask_ref[b, j : j + 1, :])
        peak = jnp.max(functools.reduce(jnp.maximum, scores), axis=0, keepdims=True)
        weights = [jnp.exp2(s - peak) for s in scores]
        norm = jnp.sum(functools.reduce(jnp.add, weights), axis=0, keepdims=True)
        total = None
        for j in range(capacity):
            term = dot_plain(vt_ref[slots_ref[b, j]], weights[j].astype(BF16))
            total = term if total is None else total + term
        part_ref[head, b] = total.astype(BF16)
        stat_ref[b, 0, pl.ds(head, 1), :] = peak
        stat_ref[b, 1, pl.ds(head, 1), :] = norm
        return carry

    lax.fori_loop(0, groups, one_block, 0)

    def part_push(h, peer, owner):
        return push(
            part_ref.at[h, peer], got_ref.at[owner, h], send.at[h, peer], recv.at[h, owner], peer
        )

    def part_keep(h):
        return pltpu.make_async_copy(part_ref.at[h, me], got_ref.at[me, h], local.at[h])

    def stat_push(peer, owner):
        return push(
            stat_ref.at[peer], gstat_ref.at[owner], ssend.at[peer], srecv.at[owner], peer
        )

    for d in range(1, groups):
        part_push(head, lax.rem(me + d, groups), me).start()
    part_keep(head).start()

    @pl.when(head == heads - 1)
    def _():
        keep = pltpu.make_async_copy(stat_ref.at[me], gstat_ref.at[me], local.at[heads])
        keep.start()
        for d in range(1, groups):
            stat_push(lax.rem(me + d, groups), me).start()

        def finish(h, carry):
            for d in range(1, groups):
                peer = lax.rem(me + d, groups)
                part_push(h, peer, me).wait_send()
                part_push(h, peer, peer).wait_recv()
            part_keep(h).wait()
            return carry

        lax.fori_loop(0, heads, finish, 0)
        for d in range(1, groups):
            peer = lax.rem(me + d, groups)
            stat_push(peer, me).wait_send()
            stat_push(peer, peer).wait_recv()
        keep.wait()


def holder_forward(slots, mask, q_all, keys, values, capacity):
    rows, width = q_all.shape
    heads, groups, stored = width // HS, rows // BLOCK, keys.shape[0]
    column = lambda n: pl.BlockSpec((n, HS), lambda h: (0, h))
    store = pl.BlockSpec((stored, BLOCK, HS), lambda h: (0, 0, h))
    fixed = lambda shape: pl.BlockSpec(shape, lambda h: (0,) * len(shape))
    anywhere = pl.BlockSpec(memory_space=pl.ANY)
    dma = pltpu.SemaphoreType.DMA
    return pl.pallas_call(
        functools.partial(forward_kernel, groups, heads, capacity, stored),
        grid=(heads,),
        in_specs=[
            pl.BlockSpec(memory_space=pltpu.SMEM),
            fixed(mask.shape), column(rows), store, store,
        ],
        out_specs=[anywhere, anywhere],
        scratch_shapes=[
            pltpu.VMEM((stored, HS, BLOCK), BF16),
            pltpu.VMEM((heads, groups, HS, BLOCK), BF16),
            pltpu.VMEM((groups, 2, STAT_ROWS, BLOCK), F32),
            dma((heads, groups)), dma((heads, groups)), dma((groups,)), dma((groups,)),
            dma((heads + 1,)),
        ],
        out_shape=[
            jax.ShapeDtypeStruct((groups, heads, HS, BLOCK), BF16),
            jax.ShapeDtypeStruct((groups, 2, STAT_ROWS, BLOCK), F32),
        ],
        compiler_params=remote_params(1),
        cost_estimate=pl.CostEstimate(flops=4 * 10**9, bytes_accessed=16 * 10**6, transcendentals=0),
    )(slots, mask, q_all, keys, values)


def combine_kernel(
    groups, heads, q_ref, k_ref, v_ref, g_ref, got_ref, stat_ref, att_ref, dq_ref, all_ref,
    row_ref, send, recv, local,
):
    head = pl.program_id(0)
    me = lax.axis_index("mem")

    @pl.when(head == 0)
    def _():
        meet(groups, me)
        row_ref[...] = jnp.zeros_like(row_ref)

    q, k, v, g = q_ref[...], k_ref[...], v_ref[...], g_ref[...]
    key_at = lax.broadcasted_iota(jnp.int32, (BLOCK, BLOCK), 0)
    query_at = lax.broadcasted_iota(jnp.int32, (BLOCK, BLOCK), 1)
    counted = key_at <= query_at
    s = dot_last(k, q) * (SCALE * LOG2E)
    s = jnp.where(counted, s, LOWEST)
    peak = jnp.max(s, axis=0, keepdims=True)
    got_peak = [stat_ref[i, 0, pl.ds(head, 1), :] for i in range(groups)]
    got_norm = [stat_ref[i, 1, pl.ds(head, 1), :] for i in range(groups)]
    peak = functools.reduce(jnp.maximum, got_peak, peak)
    w = jnp.where(counted, jnp.exp2(s - peak), 0.0)
    norm = jnp.sum(w, axis=0, keepdims=True)
    mixed = dot_plain(v.T, w.astype(BF16))
    for i in range(groups):
        factor = jnp.exp2(got_peak[i] - peak)
        norm = norm + got_norm[i] * factor
        mixed = mixed + got_ref[i, 0].astype(F32) * factor
    attention = (mixed / norm).astype(BF16)
    att_ref[...] = attention.T
    lse = peak + jnp.log2(norm)
    delta = jnp.sum(g.T.astype(F32) * attention.astype(F32), axis=0, keepdims=True)
    row_ref[0, pl.ds(head, 1), :] = lse
    row_ref[1, pl.ds(head, 1), :] = delta
    prob = jnp.where(counted, jnp.exp2(s - lse), 0.0)
    ds = (prob * (dot_last(v, g) - delta)).astype(BF16)
    dq_ref[...] = dot_plain(k.T, ds).T * SCALE

    @pl.when(head == heads - 1)
    def _():
        keep = pltpu.make_async_copy(row_ref, all_ref.at[me], local.at[0])
        keep.start()

        def row_push(peer, owner):
            return push(row_ref, all_ref.at[owner], send.at[peer], recv.at[owner], peer)

        for d in range(1, groups):
            row_push(lax.rem(me + d, groups), me).start()
        for d in range(1, groups):
            peer = lax.rem(me + d, groups)
            row_push(peer, me).wait_send()
            row_push(peer, peer).wait_recv()
        keep.wait()


def combine(query, keys, values, grad, got, stats):
    rows, width = query.shape
    heads, groups = width // HS, got.shape[0]
    column = pl.BlockSpec((rows, HS), lambda h: (0, h))
    dma = pltpu.SemaphoreType.DMA
    return pl.pallas_call(
        functools.partial(combine_kernel, groups, heads),
        grid=(heads,),
        in_specs=[
            column, column, column, column,
            pl.BlockSpec((groups, 1, HS, BLOCK), lambda h: (0, h, 0, 0)),
            pl.BlockSpec((groups, 2, STAT_ROWS, BLOCK), lambda h: (0, 0, 0, 0)),
        ],
        out_specs=[column, column, pl.BlockSpec(memory_space=pl.ANY)],
        out_shape=[
            jax.ShapeDtypeStruct((rows, width), BF16),
            jax.ShapeDtypeStruct((rows, width), F32),
            jax.ShapeDtypeStruct((groups, 2, STAT_ROWS, BLOCK), F32),
        ],
        scratch_shapes=[
            pltpu.VMEM((2, STAT_ROWS, BLOCK), F32), dma((groups,)), dma((groups,)), dma((1,)),
        ],
        compiler_params=remote_params(2),
        cost_estimate=pl.CostEstimate(flops=10**8, bytes_accessed=6 * 10**6, transcendentals=0),
    )(query, keys, values, grad, got, stats)


def backward_kernel(
    groups, heads, capacity, stored,
    slots_ref, terms_ref, mask_ref, q_ref, g_ref, k_ref, v_ref, row_ref, got_ref, dk_ref, dv_ref,
    kt_ref, dkp_ref, dvp_ref, part_ref, send, recv, local,
):
    head = pl.program_id(0)
    me = lax.axis_index("mem")

    @pl.when(head == 0)
    def _():
        meet(groups, me)
        dkp_ref[groups * capacity] = jnp.zeros((BLOCK, HS), F32)
        dvp_ref[groups * capacity] = jnp.zeros((BLOCK, HS), F32)

    for m in range(stored):
        kt_ref[m] = k_ref[m].T

    def one_block(b, carry):
        here = pl.ds(pl.multiple_of(b * BLOCK, BLOCK), BLOCK)
        q, g = q_ref[here, :], g_ref[here, :]
        lse = row_ref[b, 0, pl.ds(head, 1), :]
        delta = row_ref[b, 1, pl.ds(head, 1), :]
        total = None
        for j in range(capacity):
            s = dot_last(k_ref[slots_ref[b, j]], q) * (SCALE * LOG2E)
            s = s + mask_ref[b, j : j + 1, :]
            prob = jnp.exp2(s - lse)
            ds = (prob * (dot_last(v_ref[slots_ref[b, j]], g) - delta)).astype(BF16)
            term = dot_plain(kt_ref[slots_ref[b, j]], ds)
            total = term if total is None else total + term
            dkp_ref[b * capacity + j] = dot_plain(ds, q)
            dvp_ref[b * capacity + j] = dot_plain(prob.astype(BF16), g)
        part_ref[head, b] = (total * SCALE).T.astype(BF16)
        return carry

    lax.fori_loop(0, groups, one_block, 0)

    def part_push(h, peer, owner):
        at = pl.ds(pl.multiple_of(h * HS, HS), HS)
        return push(
            part_ref.at[h, peer], got_ref.at[owner, :, at], send.at[h, peer], recv.at[h, owner], peer
        )

    def part_keep(h):
        at = pl.ds(pl.multiple_of(h * HS, HS), HS)
        return pltpu.make_async_copy(part_ref.at[h, me], got_ref.at[me, :, at], local.at[h])

    for d in range(1, groups):
        part_push(head, lax.rem(me + d, groups), me).start()
    part_keep(head).start()

    def one_slot(m, carry):
        at = pl.ds(pl.multiple_of(m * BLOCK, BLOCK), BLOCK)
        dk = functools.reduce(jnp.add, [dkp_ref[terms_ref[m, b]] for b in range(groups)])
        dv = functools.reduce(jnp.add, [dvp_ref[terms_ref[m, b]] for b in range(groups)])
        dk_ref[at, :] = (dk * SCALE).astype(BF16)
        dv_ref[at, :] = dv.astype(BF16)
        return carry

    lax.fori_loop(0, stored, one_slot, 0)

    @pl.when(head == heads - 1)
    def _():
        def finish(h, carry):
            for d in range(1, groups):
                peer = lax.rem(me + d, groups)
                part_push(h, peer, me).wait_send()
                part_push(h, peer, peer).wait_recv()
            part_keep(h).wait()
            return carry

        lax.fori_loop(0, heads, finish, 0)


def holder_backward(slots, terms, mask, q_all, g_all, keys, values, row_stats, capacity):
    rows, width = q_all.shape
    heads, groups, stored = width // HS, rows // BLOCK, keys.shape[0]
    column = lambda n: pl.BlockSpec((n, HS), lambda h: (0, h))
    store = pl.BlockSpec((stored, BLOCK, HS), lambda h: (0, 0, h))
    fixed = lambda shape: pl.BlockSpec(shape, lambda h: (0,) * len(shape))
    mem = stored * BLOCK
    dma = pltpu.SemaphoreType.DMA
    smem = pl.BlockSpec(memory_space=pltpu.SMEM)
    return pl.pallas_call(
        functools.partial(backward_kernel, groups, heads, capacity, stored),
        grid=(heads,),
        in_specs=[
            smem, smem, fixed(mask.shape), column(rows), column(rows), store, store,
            pl.BlockSpec((groups, 2, STAT_ROWS, BLOCK), lambda h: (0, 0, 0, 0)),
        ],
        out_specs=[pl.BlockSpec(memory_space=pl.ANY), column(mem), column(mem)],
        scratch_shapes=[
            pltpu.VMEM((stored, HS, BLOCK), BF16),
            pltpu.VMEM((groups * capacity + 1, BLOCK, HS), F32),
            pltpu.VMEM((groups * capacity + 1, BLOCK, HS), F32),
            pltpu.VMEM((heads, groups, BLOCK, HS), BF16),
            dma((heads, groups)), dma((heads, groups)), dma((heads,)),
        ],
        out_shape=[
            jax.ShapeDtypeStruct((groups, BLOCK, width), BF16),
            jax.ShapeDtypeStruct((mem, width), BF16),
            jax.ShapeDtypeStruct((mem, width), BF16),
        ],
        compiler_params=remote_params(3),
        cost_estimate=pl.CostEstimate(flops=10**10, bytes_accessed=28 * 10**6, transcendentals=0),
    )(slots, terms, mask, q_all, g_all, keys, values, row_stats)


def slot_terms(slots, capacity, stored):
    blocks = slots.shape[0]
    place = jnp.arange(capacity, dtype=jnp.int32)
    pair = jnp.arange(blocks, dtype=jnp.int32)[:, None] * capacity + place[None, :]
    filled = place[None, :] < slots[:, capacity:]
    match = jnp.logical_and(
        filled[None], slots[None, :, :capacity] == jnp.arange(stored, dtype=jnp.int32)[:, None, None]
    )
    none = blocks * capacity
    return none + jnp.sum(jnp.where(match, pair[None] - none, 0), axis=2).astype(jnp.int32)


def per_device(
    query, local_keys, local_values, mem_keys, mem_values, block_ids, out_proj, grad_out
):
    groups = lax.axis_size("mem")
    holder = lax.axis_index("mem")
    stored = mem_keys.shape[0] // BLOCK
    capacity = R // groups + 2
    width = query.shape[1]
    padded = jnp.pad(block_ids, ((0, 7), (0, HS - R)))
    q_all, ids = ring_gather(query, padded, groups)
    q_all = q_all.reshape(groups * BLOCK, width)
    slots = owned_slots(ids[:, 0, :R], holder, capacity, stored)
    terms = slot_terms(slots, capacity, stored)
    grad = lax.dot_general(
        lax.all_gather(grad_out, "head", axis=1, tiled=True),
        out_proj,
        (((1,), (1,)), ((), ())),
        preferred_element_type=F32,
    ).astype(BF16)
    g_all = lax.all_gather(grad, "mem", axis=0, tiled=True)
    slots, grad = lax.optimization_barrier((slots, grad))
    filled = jnp.arange(capacity, dtype=jnp.int32)[None, :] < slots[:, capacity:]
    mask = jnp.broadcast_to(
        jnp.where(filled, 0.0, LOWEST).astype(F32)[:, :, None], (groups, capacity, BLOCK)
    )
    key_store = mem_keys.reshape(stored, BLOCK, width)
    value_store = mem_values.reshape(stored, BLOCK, width)
    got, got_stats = holder_forward(slots, mask, q_all, key_store, value_store, capacity)
    attention, local_dq, all_stats = combine(
        query, local_keys, local_values, grad, got, got_stats
    )
    projected = jnp.dot(attention, out_proj, preferred_element_type=F32).astype(BF16)
    projected, all_stats = lax.optimization_barrier((projected, all_stats))
    output = lax.psum_scatter(projected, "head", scatter_dimension=1, tiled=True)
    got_dq, grad_mem_keys, grad_mem_values = holder_backward(
        slots, terms, mask, q_all, g_all, key_store, value_store, all_stats, capacity
    )
    grad_query = (jnp.sum(got_dq.astype(F32), axis=0) + local_dq).astype(BF16)
    return (output, grad_query, grad_mem_keys, grad_mem_values)


def solution(mesh):
    split = P("mem", "head")
    placed = (split, split, split, split, split, P("mem", None), P("head", None), split)
    return jax.shard_map(
        per_device, mesh=mesh, in_specs=placed, out_specs=(split,) * 4, check_vma=False
    )
```

```python
import functools
import math

import jax
import jax.numpy as jnp
from jax import lax
from jax.experimental import pallas as pl
from jax.experimental.pallas import tpu as pltpu
from jax.sharding import PartitionSpec as P

HS = 128
BLOCK = 128
R = 32
STAT_ROWS = 16
UNROLL = 1
LOWEST = -1e30
SCALE = HS ** (-0.5)
LOG2E = math.log2(math.e)
F32 = jnp.float32
BF16 = jnp.bfloat16
MESH = pl.DeviceIdType.MESH
VMEM_LIMIT = 56 * 1024 * 1024


def dot_last(a, b):
    return lax.dot_general(a, b, (((1,), (1,)), ((), ())), preferred_element_type=F32)


def dot_plain(a, b):
    return lax.dot_general(a, b, (((1,), (0,)), ((), ())), preferred_element_type=F32)


def owned_slots(ids, holder, capacity, stored):
    is_owned = ids // stored == holder
    rank = jnp.cumsum(is_owned.astype(jnp.int32), axis=1) - 1
    chosen = jnp.logical_and(
        is_owned[:, None, :], rank[:, None, :] == jnp.arange(capacity, dtype=jnp.int32)[None, :, None]
    )
    slots = jnp.sum(jnp.where(chosen, (ids % stored)[:, None, :], 0), axis=2).astype(jnp.int32)
    count = jnp.sum(is_owned.astype(jnp.int32), axis=1, keepdims=True)
    return jnp.concatenate([slots, count], axis=1)


def meet(groups, me):
    barrier = pltpu.get_barrier_semaphore()
    for d in range(1, groups):
        pl.semaphore_signal(
            barrier, inc=1, device_id={"mem": lax.rem(me + d, groups)}, device_id_type=MESH
        )
    pl.semaphore_wait(barrier, groups - 1)


def push(src, dst, send_sem, recv_sem, peer):
    return pltpu.make_async_remote_copy(
        src_ref=src,
        dst_ref=dst,
        send_sem=send_sem,
        recv_sem=recv_sem,
        device_id={"mem": peer},
        device_id_type=MESH,
    )


def remote_params(collective_id):
    return pltpu.CompilerParams(
        vmem_limit_bytes=VMEM_LIMIT, collective_id=collective_id, has_side_effects=True
    )


def ring_kernel(groups, x_ref, i_ref, xs_ref, is_ref, local, xsend, xrecv, isend, irecv):
    me = lax.axis_index("mem")
    place = (1 - me % 2) * (me // 2) + (me % 2) * (groups - 1 - me // 2)

    def device_at(p):
        p = lax.rem(p + groups, groups)
        upper = p // (groups // 2)
        return (1 - upper) * (2 * p) + upper * (2 * (groups - 1 - p) + 1)

    sides = (device_at(place + 1), device_at(place - 1))
    barrier = pltpu.get_barrier_semaphore()
    for side in sides:
        pl.semaphore_signal(barrier, inc=1, device_id={"mem": side}, device_id_type=MESH)
    pl.semaphore_wait(barrier, 2)
    own = [
        pltpu.make_async_copy(x_ref, xs_ref.at[me], local.at[0]),
        pltpu.make_async_copy(i_ref, is_ref.at[me], local.at[1]),
    ]
    for copy in own:
        copy.start()
    steps = (groups // 2, groups - 1 - groups // 2)
    sent = []
    for t in range(steps[0]):
        for way in range(2):
            if t >= steps[way]:
                continue
            sign = 1 - 2 * way
            block = device_at(place - sign * t)
            if t:
                before = device_at(place - sign * t)
                push(x_ref, xs_ref.at[before], xsend.at[way, t - 1], xrecv.at[way, t - 1], sides[way]).wait_recv()
                push(i_ref, is_ref.at[before], isend.at[way, t - 1], irecv.at[way, t - 1], sides[way]).wait_recv()
            for src, dst, ss, rs in (
                (x_ref if t == 0 else xs_ref.at[block], xs_ref.at[block], xsend, xrecv),
                (i_ref if t == 0 else is_ref.at[block], is_ref.at[block], isend, irecv),
            ):
                copy = push(src, dst, ss.at[way, t], rs.at[way, t], sides[way])
                copy.start()
                sent.append(copy)
    for way in range(2):
        t = steps[way]
        last = device_at(place - (1 - 2 * way) * t)
        push(x_ref, xs_ref.at[last], xsend.at[way, t - 1], xrecv.at[way, t - 1], sides[way]).wait_recv()
        push(i_ref, is_ref.at[last], isend.at[way, t - 1], irecv.at[way, t - 1], sides[way]).wait_recv()
    for copy in sent:
        copy.wait_send()
    for copy in own:
        copy.wait()


def ring_gather(x, ids, groups):
    steps = groups // 2
    anywhere = pl.BlockSpec(memory_space=pl.ANY)
    return pl.pallas_call(
        functools.partial(ring_kernel, groups),
        in_specs=[anywhere, anywhere],
        out_specs=[anywhere, anywhere],
        out_shape=[
            jax.ShapeDtypeStruct((groups,) + x.shape, x.dtype),
            jax.ShapeDtypeStruct((groups,) + ids.shape, ids.dtype),
        ],
        scratch_shapes=[pltpu.SemaphoreType.DMA((2,))] + [pltpu.SemaphoreType.DMA((2, steps))] * 4,
        compiler_params=remote_params(0),
        cost_estimate=pl.CostEstimate(flops=2 * 10**10, bytes_accessed=10**8, transcendentals=0),
    )(x, ids)


def forward_kernel(
    groups, heads, capacity, stored,
    slots_ref, mask_ref, q_ref, k_ref, v_ref, got_ref, gstat_ref,
    vt_ref, part_ref, stat_ref, send, recv, ssend, srecv, local,
):
    head = pl.program_id(0)
    me = lax.axis_index("mem")

    @pl.when(head == 0)
    def _():
        meet(groups, me)
        stat_ref[...] = jnp.zeros_like(stat_ref)

    for m in range(stored):
        vt_ref[m] = v_ref[m].T

    def one_block(b, carry):
        q = q_ref[pl.ds(pl.multiple_of(b * BLOCK, BLOCK), BLOCK), :]
        keys = jnp.concatenate([k_ref[slots_ref[b, j]] for j in range(capacity)], axis=0)
        scores = dot_last(keys, q) * (SCALE * LOG2E)
        scores = scores.reshape(capacity, BLOCK, BLOCK) + mask_ref[b][:, None, :]
        peak = jnp.max(jnp.max(scores, axis=0), axis=0, keepdims=True)
        weights = jnp.exp2(scores - peak)
        norm = jnp.sum(jnp.sum(weights, axis=0), axis=0, keepdims=True)
        values = jnp.concatenate([vt_ref[slots_ref[b, j]] for j in range(capacity)], axis=1)
        total = dot_plain(values, weights.astype(BF16).reshape(capacity * BLOCK, BLOCK))
        part_ref[head, b] = total.astype(BF16)
        stat_ref[b, 0, pl.ds(head, 1), :] = peak
        stat_ref[b, 1, pl.ds(head, 1), :] = norm
        return carry

    lax.fori_loop(0, groups, one_block, 0, unroll=UNROLL)

    def part_push(h, peer, owner):
        return push(
            part_ref.at[h, peer], got_ref.at[owner, h], send.at[h, peer], recv.at[h, owner], peer
        )

    def part_keep(h):
        return pltpu.make_async_copy(part_ref.at[h, me], got_ref.at[me, h], local.at[h])

    def stat_push(peer, owner):
        return push(
            stat_ref.at[peer], gstat_ref.at[owner], ssend.at[peer], srecv.at[owner], peer
        )

    for d in range(1, groups):
        part_push(head, lax.rem(me + d, groups), me).start()
    part_keep(head).start()

    @pl.when(head == heads - 1)
    def _():
        keep = pltpu.make_async_copy(stat_ref.at[me], gstat_ref.at[me], local.at[heads])
        keep.start()
        for d in range(1, groups):
            stat_push(lax.rem(me + d, groups), me).start()

        def finish(h, carry):
            for d in range(1, groups):
                peer = lax.rem(me + d, groups)
                part_push(h, peer, me).wait_send()
                part_push(h, peer, peer).wait_recv()
            part_keep(h).wait()
            return carry

        lax.fori_loop(0, heads, finish, 0)
        for d in range(1, groups):
            peer = lax.rem(me + d, groups)
            stat_push(peer, me).wait_send()
            stat_push(peer, peer).wait_recv()
        keep.wait()


def holder_forward(slots, mask, q_all, keys, values, capacity):
    rows, width = q_all.shape
    heads, groups, stored = width // HS, rows // BLOCK, keys.shape[0]
    column = lambda n: pl.BlockSpec((n, HS), lambda h: (0, h))
    store = pl.BlockSpec((stored, BLOCK, HS), lambda h: (0, 0, h))
    fixed = lambda shape: pl.BlockSpec(shape, lambda h: (0,) * len(shape))
    anywhere = pl.BlockSpec(memory_space=pl.ANY)
    dma = pltpu.SemaphoreType.DMA
    return pl.pallas_call(
        functools.partial(forward_kernel, groups, heads, capacity, stored),
        grid=(heads,),
        in_specs=[
            pl.BlockSpec(memory_space=pltpu.SMEM),
            fixed(mask.shape), column(rows), store, store,
        ],
        out_specs=[anywhere, anywhere],
        scratch_shapes=[
            pltpu.VMEM((stored, HS, BLOCK), BF16),
            pltpu.VMEM((heads, groups, HS, BLOCK), BF16),
            pltpu.VMEM((groups, 2, STAT_ROWS, BLOCK), F32),
            dma((heads, groups)), dma((heads, groups)), dma((groups,)), dma((groups,)),
            dma((heads + 1,)),
        ],
        out_shape=[
            jax.ShapeDtypeStruct((groups, heads, HS, BLOCK), BF16),
            jax.ShapeDtypeStruct((groups, 2, STAT_ROWS, BLOCK), F32),
        ],
        compiler_params=remote_params(1),
        cost_estimate=pl.CostEstimate(flops=4 * 10**9, bytes_accessed=16 * 10**6, transcendentals=0),
    )(slots, mask, q_all, keys, values)


def combine_kernel(
    groups, heads, q_ref, k_ref, v_ref, g_ref, got_ref, stat_ref, att_ref, dq_ref, all_ref,
    row_ref, send, recv, local,
):
    head = pl.program_id(0)
    me = lax.axis_index("mem")

    @pl.when(head == 0)
    def _():
        meet(groups, me)
        row_ref[...] = jnp.zeros_like(row_ref)

    q, k, v, g = q_ref[...], k_ref[...], v_ref[...], g_ref[...]
    key_at = lax.broadcasted_iota(jnp.int32, (BLOCK, BLOCK), 0)
    query_at = lax.broadcasted_iota(jnp.int32, (BLOCK, BLOCK), 1)
    counted = key_at <= query_at
    s = dot_last(k, q) * (SCALE * LOG2E)
    s = jnp.where(counted, s, LOWEST)
    peak = jnp.max(s, axis=0, keepdims=True)
    got_peak = [stat_ref[i, 0, pl.ds(head, 1), :] for i in range(groups)]
    got_norm = [stat_ref[i, 1, pl.ds(head, 1), :] for i in range(groups)]
    peak = functools.reduce(jnp.maximum, got_peak, peak)
    w = jnp.where(counted, jnp.exp2(s - peak), 0.0)
    norm = jnp.sum(w, axis=0, keepdims=True)
    mixed = dot_plain(v.T, w.astype(BF16))
    for i in range(groups):
        factor = jnp.exp2(got_peak[i] - peak)
        norm = norm + got_norm[i] * factor
        mixed = mixed + got_ref[i, 0].astype(F32) * factor
    attention = (mixed / norm).astype(BF16)
    att_ref[...] = attention.T
    lse = peak + jnp.log2(norm)
    delta = jnp.sum(g.T.astype(F32) * attention.astype(F32), axis=0, keepdims=True)
    row_ref[0, pl.ds(head, 1), :] = lse
    row_ref[1, pl.ds(head, 1), :] = delta
    prob = jnp.where(counted, jnp.exp2(s - lse), 0.0)
    ds = (prob * (dot_last(v, g) - delta)).astype(BF16)
    dq_ref[...] = dot_plain(k.T, ds).T * SCALE

    @pl.when(head == heads - 1)
    def _():
        keep = pltpu.make_async_copy(row_ref, all_ref.at[me], local.at[0])
        keep.start()

        def row_push(peer, owner):
            return push(row_ref, all_ref.at[owner], send.at[peer], recv.at[owner], peer)

        for d in range(1, groups):
            row_push(lax.rem(me + d, groups), me).start()
        for d in range(1, groups):
            peer = lax.rem(me + d, groups)
            row_push(peer, me).wait_send()
            row_push(peer, peer).wait_recv()
        keep.wait()


def combine(query, keys, values, grad, got, stats):
    rows, width = query.shape
    heads, groups = width // HS, got.shape[0]
    column = pl.BlockSpec((rows, HS), lambda h: (0, h))
    dma = pltpu.SemaphoreType.DMA
    return pl.pallas_call(
        functools.partial(combine_kernel, groups, heads),
        grid=(heads,),
        in_specs=[
            column, column, column, column,
            pl.BlockSpec((groups, 1, HS, BLOCK), lambda h: (0, h, 0, 0)),
            pl.BlockSpec((groups, 2, STAT_ROWS, BLOCK), lambda h: (0, 0, 0, 0)),
        ],
        out_specs=[column, column, pl.BlockSpec(memory_space=pl.ANY)],
        out_shape=[
            jax.ShapeDtypeStruct((rows, width), BF16),
            jax.ShapeDtypeStruct((rows, width), F32),
            jax.ShapeDtypeStruct((groups, 2, STAT_ROWS, BLOCK), F32),
        ],
        scratch_shapes=[
            pltpu.VMEM((2, STAT_ROWS, BLOCK), F32), dma((groups,)), dma((groups,)), dma((1,)),
        ],
        compiler_params=remote_params(2),
        cost_estimate=pl.CostEstimate(flops=10**8, bytes_accessed=6 * 10**6, transcendentals=0),
    )(query, keys, values, grad, got, stats)


def backward_kernel(
    groups, heads, capacity, stored,
    slots_ref, terms_ref, mask_ref, q_ref, g_ref, k_ref, v_ref, row_ref, got_ref, dk_ref, dv_ref,
    kt_ref, dkp_ref, dvp_ref, part_ref, send, recv, local,
):
    head = pl.program_id(0)
    me = lax.axis_index("mem")

    @pl.when(head == 0)
    def _():
        meet(groups, me)
        dkp_ref[groups * capacity] = jnp.zeros((BLOCK, HS), F32)
        dvp_ref[groups * capacity] = jnp.zeros((BLOCK, HS), F32)

    for m in range(stored):
        kt_ref[m] = k_ref[m].T

    def one_block(b, carry):
        here = pl.ds(pl.multiple_of(b * BLOCK, BLOCK), BLOCK)
        q, g = q_ref[here, :], g_ref[here, :]
        lse = row_ref[b, 0, pl.ds(head, 1), :]
        delta = row_ref[b, 1, pl.ds(head, 1), :]
        picked = [slots_ref[b, j] for j in range(capacity)]
        keys = jnp.concatenate([k_ref[slot] for slot in picked], axis=0)
        values = jnp.concatenate([v_ref[slot] for slot in picked], axis=0)
        scores = dot_last(keys, q) * (SCALE * LOG2E)
        scores = scores.reshape(capacity, BLOCK, BLOCK) + mask_ref[b][:, None, :]
        prob = jnp.exp2(scores - lse)
        dprob = dot_last(values, g).reshape(capacity, BLOCK, BLOCK)
        ds = (prob * (dprob - delta)).astype(BF16).reshape(capacity * BLOCK, BLOCK)
        turned = jnp.concatenate([kt_ref[slot] for slot in picked], axis=1)
        total = dot_plain(turned, ds)
        pairs = pl.ds(b * capacity, capacity)
        shape = (capacity, BLOCK, HS)
        dkp_ref[pairs] = dot_plain(ds, q).reshape(shape)
        dvp_ref[pairs] = dot_plain(prob.astype(BF16).reshape(capacity * BLOCK, BLOCK), g).reshape(shape)
        part_ref[head, b] = (total * SCALE).T.astype(BF16)
        return carry

    lax.fori_loop(0, groups, one_block, 0, unroll=UNROLL)

    def part_push(h, peer, owner):
        at = pl.ds(pl.multiple_of(h * HS, HS), HS)
        return push(
            part_ref.at[h, peer], got_ref.at[owner, :, at], send.at[h, peer], recv.at[h, owner], peer
        )

    def part_keep(h):
        at = pl.ds(pl.multiple_of(h * HS, HS), HS)
        return pltpu.make_async_copy(part_ref.at[h, me], got_ref.at[me, :, at], local.at[h])

    for d in range(1, groups):
        part_push(head, lax.rem(me + d, groups), me).start()
    part_keep(head).start()

    def one_slot(m, carry):
        at = pl.ds(pl.multiple_of(m * BLOCK, BLOCK), BLOCK)
        dk = functools.reduce(jnp.add, [dkp_ref[terms_ref[m, b]] for b in range(groups)])
        dv = functools.reduce(jnp.add, [dvp_ref[terms_ref[m, b]] for b in range(groups)])
        dk_ref[at, :] = (dk * SCALE).astype(BF16)
        dv_ref[at, :] = dv.astype(BF16)
        return carry

    lax.fori_loop(0, stored, one_slot, 0)

    @pl.when(head == heads - 1)
    def _():
        def finish(h, carry):
            for d in range(1, groups):
                peer = lax.rem(me + d, groups)
                part_push(h, peer, me).wait_send()
                part_push(h, peer, peer).wait_recv()
            part_keep(h).wait()
            return carry

        lax.fori_loop(0, heads, finish, 0)


def holder_backward(slots, terms, mask, q_all, g_all, keys, values, row_stats, capacity):
    rows, width = q_all.shape
    heads, groups, stored = width // HS, rows // BLOCK, keys.shape[0]
    column = lambda n: pl.BlockSpec((n, HS), lambda h: (0, h))
    store = pl.BlockSpec((stored, BLOCK, HS), lambda h: (0, 0, h))
    fixed = lambda shape: pl.BlockSpec(shape, lambda h: (0,) * len(shape))
    mem = stored * BLOCK
    dma = pltpu.SemaphoreType.DMA
    smem = pl.BlockSpec(memory_space=pltpu.SMEM)
    return pl.pallas_call(
        functools.partial(backward_kernel, groups, heads, capacity, stored),
        grid=(heads,),
        in_specs=[
            smem, smem, fixed(mask.shape), column(rows), column(rows), store, store,
            pl.BlockSpec((groups, 2, STAT_ROWS, BLOCK), lambda h: (0, 0, 0, 0)),
        ],
        out_specs=[pl.BlockSpec(memory_space=pl.ANY), column(mem), column(mem)],
        scratch_shapes=[
            pltpu.VMEM((stored, HS, BLOCK), BF16),
            pltpu.VMEM((groups * capacity + 1, BLOCK, HS), F32),
            pltpu.VMEM((groups * capacity + 1, BLOCK, HS), F32),
            pltpu.VMEM((heads, groups, BLOCK, HS), BF16),
            dma((heads, groups)), dma((heads, groups)), dma((heads,)),
        ],
        out_shape=[
            jax.ShapeDtypeStruct((groups, BLOCK, width), BF16),
            jax.ShapeDtypeStruct((mem, width), BF16),
            jax.ShapeDtypeStruct((mem, width), BF16),
        ],
        compiler_params=remote_params(3),
        cost_estimate=pl.CostEstimate(flops=10**10, bytes_accessed=28 * 10**6, transcendentals=0),
    )(slots, terms, mask, q_all, g_all, keys, values, row_stats)


def slot_terms(slots, capacity, stored):
    blocks = slots.shape[0]
    place = jnp.arange(capacity, dtype=jnp.int32)
    pair = jnp.arange(blocks, dtype=jnp.int32)[:, None] * capacity + place[None, :]
    filled = place[None, :] < slots[:, capacity:]
    match = jnp.logical_and(
        filled[None], slots[None, :, :capacity] == jnp.arange(stored, dtype=jnp.int32)[:, None, None]
    )
    none = blocks * capacity
    return none + jnp.sum(jnp.where(match, pair[None] - none, 0), axis=2).astype(jnp.int32)


def per_device(
    query, local_keys, local_values, mem_keys, mem_values, block_ids, out_proj, grad_out
):
    groups = lax.axis_size("mem")
    holder = lax.axis_index("mem")
    stored = mem_keys.shape[0] // BLOCK
    capacity = R // groups + 2
    width = query.shape[1]
    padded = jnp.pad(block_ids, ((0, 7), (0, HS - R)))
    q_all, ids = ring_gather(query, padded, groups)
    q_all = q_all.reshape(groups * BLOCK, width)
    slots = owned_slots(ids[:, 0, :R], holder, capacity, stored)
    terms = slot_terms(slots, capacity, stored)
    whole_grad_out = lax.all_gather(grad_out, "head", axis=1, tiled=True)
    q_all, whole_grad_out = lax.optimization_barrier((q_all, whole_grad_out))
    grad = lax.dot_general(
        whole_grad_out,
        out_proj,
        (((1,), (1,)), ((), ())),
        preferred_element_type=F32,
    ).astype(BF16)
    g_all = lax.all_gather(grad, "mem", axis=0, tiled=True)
    slots, grad = lax.optimization_barrier((slots, grad))
    filled = jnp.arange(capacity, dtype=jnp.int32)[None, :] < slots[:, capacity:]
    mask = jnp.broadcast_to(
        jnp.where(filled, 0.0, LOWEST).astype(F32)[:, :, None], (groups, capacity, BLOCK)
    )
    key_store = mem_keys.reshape(stored, BLOCK, width)
    value_store = mem_values.reshape(stored, BLOCK, width)
    got, got_stats = holder_forward(slots, mask, q_all, key_store, value_store, capacity)
    attention, local_dq, all_stats = combine(
        query, local_keys, local_values, grad, got, got_stats
    )
    projected = jnp.dot(attention, out_proj, preferred_element_type=F32).astype(BF16)
    projected, all_stats = lax.optimization_barrier((projected, all_stats))
    output = lax.psum_scatter(projected, "head", scatter_dimension=1, tiled=True)
    got_dq, grad_mem_keys, grad_mem_values = holder_backward(
        slots, terms, mask, q_all, g_all, key_store, value_store, all_stats, capacity
    )
    grad_query = (jnp.sum(got_dq.astype(F32), axis=0) + local_dq).astype(BF16)
    return (output, grad_query, grad_mem_keys, grad_mem_values)


def solution(mesh):
    split = P("mem", "head")
    placed = (split, split, split, split, split, P("mem", None), P("head", None), split)
    return jax.shard_map(
        per_device, mesh=mesh, in_specs=placed, out_specs=(split,) * 4, check_vma=False
    )
```
